32 devices in a mesh: dp: 16 (over z, x, core), tensor: 2 (over y).
Axes of the slice: x: 2, y: 2, z: 4, core: 2. Of those that a mesh axis runs over, the one named last changes fastest.
Arguments:
- tokens: bfloat16 [32768, 1024], P(('dp', 'tensor')), may hold values from -6 to 6
- cotangent: bfloat16 [32768, 1024], P(('dp', 'tensor')), may hold values from -6 to 6
- sequence_lengths: int32 [16, 2], P('dp'), may hold values from 0 to 2048, as said below
- sequence_starts: int32 [16, 2], P('dp'), may hold values from 0 to 2048, as said below
- weight_query: float32 [1024, 1024], P('dp', 'tensor'), may hold values from -0.1875 to 0.1875
- weight_key: float32 [1024, 1024], P('dp', 'tensor'), may hold values from -0.1875 to 0.1875
- weight_value: float32 [1024, 1024], P('dp', 'tensor'), may hold values from -0.1875 to 0.1875
- weight_dense: float32 [1024, 1024], P('dp', 'tensor'), may hold values from -2 to 2
- weight_in: float32 [1024, 4096], P('dp', 'tensor'), may hold values from -0.1875 to 0.1875
- weight_out: float32 [1024, 4096], P('dp', 'tensor'), may hold values from -0.09375 to 0.09375
- vectors: float32 [1024, 13], P('dp'), may hold values from -0.8 to 1.5, as said below
- first_query: float32 [1024, 1024], P('dp', 'tensor'), may hold values from -96 to 96
- first_key: float32 [1024, 1024], P('dp', 'tensor'), may hold values from -96 to 96
- first_value: float32 [1024, 1024], P('dp', 'tensor'), may hold values from -96 to 96
- first_dense: float32 [1024, 1024], P('dp', 'tensor'), may hold values from -8 to 8
- first_in: float32 [1024, 4096], P('dp', 'tensor'), may hold values from -32 to 32
- first_out: float32 [1024, 4096], P('dp', 'tensor'), may hold values from -80 to 80
- first_vectors: float32 [1024, 13], P('dp'), may hold values from -114.04218 to 114.04218
- second_query: float32 [1024, 1024], P('dp', 'tensor'), may hold values from 1114.112 to 4423.68
- second_key: float32 [1024, 1024], P('dp', 'tensor'), may hold values from 1114.112 to 4423.68
- second_value: float32 [1024, 1024], P('dp', 'tensor'), may hold values from 1114.112 to 4423.68
- second_dense: float32 [1024, 1024], P('dp', 'tensor'), may hold values from 8.416 to 33.6
- second_in: float32 [1024, 4096], P('dp', 'tensor'), may hold values from 154.0096 to 622.592
- second_out: float32 [1024, 4096], P('dp', 'tensor'), may hold values from 720.896 to 2916.352
- second_vectors: float32 [1024, 13], P('dp'), may hold values from 154.0096 to 13762.56
Outputs:
- output: bfloat16 [32768, 1024], P(('dp', 'tensor'))
- input_grad: bfloat16 [32768, 1024], P(('dp', 'tensor'))
- next_first_query: float32 [1024, 1024], P('dp', 'tensor')
- next_first_key: float32 [1024, 1024], P('dp', 'tensor')
- next_first_value: float32 [1024, 1024], P('dp', 'tensor')
- next_first_dense: float32 [1024, 1024], P('dp', 'tensor')
- next_first_in: float32 [1024, 4096], P('dp', 'tensor')
- next_first_out: float32 [1024, 4096], P('dp', 'tensor')
- next_first_vectors: float32 [1024, 13], P('dp')
- next_second_query: float32 [1024, 1024], P('dp', 'tensor')
- next_second_key: float32 [1024, 1024], P('dp', 'tensor')
- next_second_value: float32 [1024, 1024], P('dp', 'tensor')
- next_second_dense: float32 [1024, 1024], P('dp', 'tensor')
- next_second_in: float32 [1024, 4096], P('dp', 'tensor')
- next_second_out: float32 [1024, 4096], P('dp', 'tensor')
- next_second_vectors: float32 [1024, 13], P('dp')
- next_weight_query: float32 [1024, 1024], P('dp', 'tensor')
- next_weight_key: float32 [1024, 1024], P('dp', 'tensor')
- next_weight_value: float32 [1024, 1024], P('dp', 'tensor')
- next_weight_dense: float32 [1024, 1024], P('dp', 'tensor')
- next_weight_in: float32 [1024, 4096], P('dp', 'tensor')
- next_weight_out: float32 [1024, 4096], P('dp', 'tensor')
- next_vectors: float32 [1024, 13], P('dp')
The draws below stay inside these ranges and needn't reach their ends.
Inputs may be any that keep to these rules, and one draw needn't show every extreme that they name: `sequence_lengths`: in each group the sequences occupy disjoint slots within its 2048 rows, the second after the first; the first covers rows 1023 and 1024; a length 0 marks an unused slot; some group holds a single sequence of 2048. `sequence_starts`: the offsets that go with sequence_lengths. `vectors`: gains in columns 0 and 2, biases elsewhere.
All inputs are finite; a program needn't handle non-finite values.
Results may differ from the reference program's by a relative error of at most 0.012.
The reference program's roundings to bfloat16 on the way count: a program that leaves them out, or rounds other values in their place, can miss the bound.
Values may be sent and summed in bfloat16 or wider, within the bound.
A program may use at most 320 MiB of HBM per device.

```python
import math
import jax
import jax.numpy as jnp
from jax import lax

D = 1024
HEADS = 16
HEAD_DIM = 64
ROT = 16
FF = 4096
GROUP_TOK = 2048
STEP = 10
VEC = 13
TOKENS = 32768
N_DP = 16


def pack_layout(key):
    keys = jax.random.split(key, 5)
    slots_all = GROUP_TOK
    start = jax.random.randint(keys[0], (N_DP,), 0, slots_all // 8 + 1)
    first = jax.random.randint(keys[1], (N_DP,), slots_all // 2 + 1, slots_all - start + 1)
    spacer = jax.random.randint(keys[2], (N_DP,), 0, slots_all // 16 + 1)
    later = jnp.minimum(start + first + spacer, slots_all)
    second = jax.random.randint(keys[3], (N_DP,), 0, slots_all - later + 1)
    chosen = jax.random.randint(keys[4], (), 0, N_DP)
    whole = jnp.arange(N_DP) == chosen
    start = jnp.where(whole, 0, start)
    first = jnp.where(whole, slots_all, first)
    later = jnp.where(whole, slots_all, later)
    second = jnp.where(whole, 0, second)
    lengths = jnp.stack([first, second], axis=1).astype(jnp.int32)
    offsets = jnp.stack([start, later], axis=1).astype(jnp.int32)
    return (lengths, offsets)


def draw_sequence_lengths(key, part):
    return pack_layout(key)[0]


def draw_sequence_starts(key, part):
    return pack_layout(key)[1]


def column_scale():
    factors = [1.4, 1.4, 0.6, 0.6, 1.0, 1.0, 0.8, 0.8, 0.8] + [0.3] * (FF // D)
    return jnp.array(factors, jnp.float32) * (GROUP_TOK * N_DP) ** 0.5


def draw_vectors(key, part):
    key = jax.random.fold_in(key, 13)
    keys = jax.random.split(key, 2)
    gain_cols = (jnp.arange(VEC) == 0) | (jnp.arange(VEC) == 2)
    gains = jax.random.uniform(keys[0], (D, VEC), jnp.float32, 0.6, 1.4)
    biases = 0.2 * jnp.clip(jax.random.normal(keys[1], (D, VEC), jnp.float32), -4.0, 4.0)
    return jnp.where(gain_cols[None, :], gains, biases).astype(jnp.float32)


def draw_first_vectors(key, part):
    key = jax.random.fold_in(key, 11)
    values = jnp.clip(jax.random.normal(key, (D, VEC), jnp.float32), -4.0, 4.0)
    return (values * 0.111 * column_scale()[None, :]).astype(jnp.float32)


def draw_second_vectors(key, part):
    key = jax.random.fold_in(key, 12)
    factor = jnp.exp(jax.random.uniform(key, (D, VEC), jnp.float32, 0.0, math.log(4.0)))
    scales = column_scale()
    return (factor * 0.0526 * (scales * scales)[None, :]).astype(jnp.float32)


def level_of(key, extent, shards, least, top_value):
    def one(axis_at, shards_of):
        draws = jax.random.uniform(jax.random.fold_in(jax.random.fold_in(key, 6), axis_at), (shards_of,), jnp.float32, least / len(shards), top_value / len(shards))
        return jnp.repeat(jnp.exp(draws), extent[axis_at] // shards_of).reshape((-1,) + (1,) * (len(extent) - axis_at - 1))

    level = one(*shards[0])
    for cut in shards[1:]:
        level = level * one(*cut)
    return level


def bell_draw(key, dims, deviation, bound, cuts=(), held_as=jnp.bfloat16):
    values = jax.random.normal(key, dims, jnp.float32) * deviation
    if len(cuts) > 0:
        values = level_of(key, dims, cuts, -0.22, 0.18) * values
    return jnp.clip(values, min=-bound, max=bound).astype(held_as)


def setup_inputs(seed: int = 0) -> dict:
    arg_keys = jax.random.split(jax.random.key(seed), 26)
    tokens = bell_draw(arg_keys[0], (TOKENS, D), 1.0, 6.0, ((0, 32),))
    cotangent = bell_draw(arg_keys[1], (TOKENS, D), 1.0, 6.0, ((0, 32),))
    sequence_lengths = draw_sequence_lengths(jax.random.fold_in(arg_keys[25], 71), 0)
    sequence_starts = draw_sequence_starts(jax.random.fold_in(arg_keys[25], 71), 0)
    weight_query = bell_draw(arg_keys[4], (D, D), D ** -0.5, 0.1875, ((0, 16), (1, 2)), jnp.float32)
    weight_key = bell_draw(arg_keys[5], (D, D), D ** -0.5, 0.1875, ((0, 16), (1, 2)), jnp.float32)
    weight_value = bell_draw(arg_keys[6], (D, D), D ** -0.5, 0.1875, ((0, 16), (1, 2)), jnp.float32)
    weight_dense = bell_draw(arg_keys[7], (D, D), (D * 16 // GROUP_TOK) ** -0.5, 2.0, ((0, 16), (1, 2)), jnp.float32)
    weight_in = bell_draw(arg_keys[8], (D, FF), D ** -0.5, 0.1875, ((0, 16), (1, 2)), jnp.float32)
    weight_out = bell_draw(arg_keys[9], (D, FF), FF ** -0.5, 0.09375, ((0, 16), (1, 2)), jnp.float32)
    vectors = draw_vectors(jax.random.fold_in(arg_keys[25], 71), 0)
    first_query = bell_draw(arg_keys[11], (D, D), (0.09 * (GROUP_TOK * N_DP) ** 0.5), 96.0, ((0, 16), (1, 2)), jnp.float32)
    first_key = bell_draw(arg_keys[12], (D, D), (0.09 * (GROUP_TOK * N_DP) ** 0.5), 96.0, ((0, 16), (1, 2)), jnp.float32)
    first_value = bell_draw(arg_keys[13], (D, D), (0.09 * (GROUP_TOK * N_DP) ** 0.5), 96.0, ((0, 16), (1, 2)), jnp.float32)
    first_dense = bell_draw(arg_keys[14], (D, D), (0.111 * (10 * N_DP) ** 0.5), 8.0, ((0, 16), (1, 2)), jnp.float32)
    first_in = bell_draw(arg_keys[15], (D, FF), (0.033 * (GROUP_TOK * N_DP) ** 0.5), 32.0, ((0, 16), (1, 2)), jnp.float32)
    first_out = bell_draw(arg_keys[16], (D, FF), (0.072 * (GROUP_TOK * N_DP) ** 0.5), 80.0, ((0, 16), (1, 2)), jnp.float32)
    first_vectors = draw_first_vectors(jax.random.fold_in(arg_keys[25], 71), 0)
    second_query = jnp.clip(jnp.exp(math.log(4423.68) - 1.3789142 * jax.random.uniform(arg_keys[18], (D, D), jnp.float32) ** level_of(arg_keys[18], (D, D), ((0, 16), (1, 2)), -0.2, 0.2)), 1114.112, 4423.68)
    second_key = jnp.clip(jnp.exp(math.log(4423.68) - 1.3789142 * jax.random.uniform(arg_keys[19], (D, D), jnp.float32) ** level_of(arg_keys[19], (D, D), ((0, 16), (1, 2)), -0.2, 0.2)), 1114.112, 4423.68)
    second_value = jnp.clip(jnp.exp(math.log(4423.68) - 1.3789142 * jax.random.uniform(arg_keys[20], (D, D), jnp.float32) ** level_of(arg_keys[20], (D, D), ((0, 16), (1, 2)), -0.2, 0.2)), 1114.112, 4423.68)
    second_dense = jnp.clip(jnp.exp(math.log(33.6) - 1.3843913 * jax.random.uniform(arg_keys[21], (D, D), jnp.float32) ** level_of(arg_keys[21], (D, D), ((0, 16), (1, 2)), -0.2, 0.2)), 8.416, 33.6)
    second_in = jnp.clip(jnp.exp(math.log(622.592) - 1.3968765 * jax.random.uniform(arg_keys[22], (D, FF), jnp.float32) ** level_of(arg_keys[22], (D, FF), ((0, 16), (1, 2)), -0.2, 0.2)), 154.0096, 622.592)
    second_out = jnp.clip(jnp.exp(math.log(2916.352) - 1.397594 * jax.random.uniform(arg_keys[23], (D, FF), jnp.float32) ** level_of(arg_keys[23], (D, FF), ((0, 16), (1, 2)), -0.2, 0.2)), 720.896, 2916.352)
    second_vectors = draw_second_vectors(jax.random.fold_in(arg_keys[25], 71), 0)
    return {"tokens": tokens, "cotangent": cotangent, "sequence_lengths": sequence_lengths, "sequence_starts": sequence_starts, "weight_query": weight_query, "weight_key": weight_key, "weight_value": weight_value, "weight_dense": weight_dense, "weight_in": weight_in, "weight_out": weight_out, "vectors": vectors, "first_query": first_query, "first_key": first_key, "first_value": first_value, "first_dense": first_dense, "first_in": first_in, "first_out": first_out, "first_vectors": first_vectors, "second_query": second_query, "second_key": second_key, "second_value": second_value, "second_dense": second_dense, "second_in": second_in, "second_out": second_out, "second_vectors": second_vectors}


@jax.custom_vjp
def low(v):
    return lax.optimization_barrier(v.astype(jnp.bfloat16)).astype(jnp.float32)

@jax.custom_vjp
def low_back(v):
    return v

def low_keep(v):
    return (low(v), None)

def low_pass(kept, grad):
    return (grad,)

def back_keep(v):
    return (v, None)

def back_low(kept, grad):
    return (low(grad),)
low.defvjp(low_keep, low_pass)
low_back.defvjp(back_keep, back_low)
NORM_EPS = 1e-05
BETA_FIRST = 0.9
BETA_SECOND = 0.95
ADAM_EPS = 1e-08
WEIGHT_DECAY = 0.01
RATE_MATRIX = 0.04
RATE_DENSE = 0.2
RATE_VECTOR = 0.5
MASKED = -1000000000.0
HIGHEST = lax.Precision.HIGHEST

def layout(lengths, offsets, total_rows):
    row_ids = jnp.arange(total_rows, dtype=jnp.int32)
    inside = ((row_ids[:, None] >= offsets[None, :]) & (row_ids[:, None] < offsets[None, :] + lengths[None, :])).astype(jnp.int32)
    slot_ids = jnp.arange(lengths.shape[0], dtype=jnp.int32)
    member = lax.optimization_barrier(jnp.sum(inside, axis=1))
    segment = jnp.where(member > 0, lax.optimization_barrier(jnp.sum(inside * slot_ids[None, :], axis=1)), lengths.shape[0] + row_ids)
    position = jnp.where(member > 0, row_ids - lax.optimization_barrier(jnp.sum(inside * offsets[None, :], axis=1)), 0)
    return (segment.astype(jnp.int32), position.astype(jnp.int32))

def rotate(heads, position):
    half = ROT // 2
    freq = 10000.0 ** (-2.0 * jnp.arange(half, dtype=jnp.float32) / ROT)
    angle = position.astype(jnp.float32)[:, None] * freq[None, :]
    cosine = jnp.cos(angle)[:, None, :]
    sine = jnp.sin(angle)[:, None, :]
    lower = heads[..., :half]
    upper = heads[..., half:ROT]
    return jnp.concatenate([lower * cosine - upper * sine, upper * cosine + lower * sine, heads[..., ROT:]], axis=-1)

def layer_norm(values, gain, shift):
    centred = values - lax.optimization_barrier(jnp.mean(values, axis=-1, keepdims=True))
    spread = lax.optimization_barrier(jnp.mean(centred * centred, axis=-1, keepdims=True))
    return centred * lax.rsqrt(spread + NORM_EPS) * gain + shift

def attention(query_rows, key_rows, value_rows, segment):
    total_rows = query_rows.shape[0]
    block_rows = min(512, total_rows)
    score_scale = HEAD_DIM ** (-0.5)
    columns = jnp.arange(total_rows, dtype=jnp.int32)

    def one_block(start):
        query_block = lax.dynamic_slice_in_dim(query_rows, start, block_rows, 0)
        block_segment = lax.dynamic_slice_in_dim(segment, start, block_rows, 0)
        block_ids = start + jnp.arange(block_rows, dtype=jnp.int32)
        scores = low_back(jnp.einsum('qhd,khd->hqk', query_block, key_rows, precision=HIGHEST) * score_scale)
        allowed = (block_segment[:, None] == segment[None, :]) & (columns[None, :] <= block_ids[:, None])
        scores = jnp.where(allowed[None], scores, MASKED)
        row_max = lax.optimization_barrier(jnp.max(scores, axis=-1, keepdims=True))
        weights = jnp.exp(scores - row_max)
        probs = weights / lax.optimization_barrier(jnp.sum(weights, axis=-1, keepdims=True))
        return jnp.einsum('hqk,khd->qhd', low(probs), value_rows, precision=HIGHEST)
    starts = jnp.arange(total_rows // block_rows, dtype=jnp.int32) * block_rows
    blocks = lax.map(jax.checkpoint(one_block), starts)
    return blocks.reshape(total_rows, -1)

def forward(layer_in, weight_query, weight_key, weight_value, weight_dense, weight_in, weight_out, vectors, segment, position):
    total_rows = layer_in.shape[0]
    vector_copy = low(vectors)
    columns = [vector_copy[:, column] for column in range(9)]
    gain_one, shift_one, gain_two, shift_two, bias_dense, bias_out, bias_query, bias_key, bias_value = columns
    bias_in = vector_copy[:, 9:].T.reshape(-1)
    normed_one = low(layer_norm(layer_in, gain_one, shift_one))
    normed_two = low(layer_norm(layer_in, gain_two, shift_two))

    def project(weight_matrix, bias):
        return (jnp.dot(normed_one, low(weight_matrix), precision=HIGHEST) + bias).reshape(total_rows, HEADS, HEAD_DIM)
    query_rows = low(rotate(low_back(project(weight_query, bias_query)), position))
    key_rows = low(rotate(low_back(project(weight_key, bias_key)), position))
    value_rows = low(low_back(project(weight_value, bias_value)))
    attended = low(low_back(attention(query_rows, key_rows, value_rows, segment)))
    attn_branch = jnp.dot(attended, low(weight_dense).T, precision=HIGHEST)
    hidden_pre = low_back(jnp.dot(normed_two, low(weight_in), precision=HIGHEST) + bias_in)
    activated = low(jax.nn.gelu(hidden_pre, approximate=False))
    mlp_branch = jnp.dot(activated, low(weight_out).T, precision=HIGHEST)
    return layer_in + attn_branch + mlp_branch + bias_dense + bias_out

def adam_update(weight_matrix, grad, first, second, rate, decay):
    first = BETA_FIRST * first + (1.0 - BETA_FIRST) * grad
    second = BETA_SECOND * second + (1.0 - BETA_SECOND) * grad * grad
    fixed_first = first / (1.0 - BETA_FIRST ** STEP)
    fixed_second = second / (1.0 - BETA_SECOND ** STEP)
    weight_matrix = weight_matrix - rate * (fixed_first / (jnp.sqrt(fixed_second) + ADAM_EPS) + decay * weight_matrix)
    return (first, second, weight_matrix)

def reference(tokens, cotangent, sequence_lengths, sequence_starts, weight_query, weight_key, weight_value, weight_dense, weight_in, weight_out, vectors, first_query, first_key, first_value, first_dense, first_in, first_out, first_vectors, second_query, second_key, second_value, second_dense, second_in, second_out, second_vectors):
    parameter_set = (weight_query, weight_key, weight_value, weight_dense, weight_in, weight_out, vectors)
    input_per_group = tokens.astype(jnp.float32).reshape(N_DP, GROUP_TOK, D)
    gradient_per_group = cotangent.astype(jnp.float32).reshape(N_DP, GROUP_TOK, D)

    def step_per_group(summed_total, group_item):
        layer_in, grad_rows, lengths, offsets = group_item
        segment, position = layout(lengths, offsets, GROUP_TOK)

        def apply(inner, w_one, w_two, w_three, w_four, w_five, w_six, w_seven):
            return forward(inner, w_one, w_two, w_three, w_four, w_five, w_six, w_seven, segment, position)
        result, pullback = jax.vjp(apply, layer_in, weight_query, weight_key, weight_value, weight_dense, weight_in, weight_out, vectors)
        grads = pullback(grad_rows)
        summed_total = tuple((before + fresh for before, fresh in zip(summed_total, grads[1:])))
        return (summed_total, (result.astype(jnp.bfloat16), grads[0].astype(jnp.bfloat16)))
    empty_slots_list = tuple((jnp.zeros_like(weight_matrix) for weight_matrix in parameter_set))
    summed_total, (output_list, incoming_gradient) = lax.scan(step_per_group, empty_slots_list, (input_per_group, gradient_per_group, sequence_lengths, sequence_starts))
    firsts = (first_query, first_key, first_value, first_dense, first_in, first_out, first_vectors)
    seconds = (second_query, second_key, second_value, second_dense, second_in, second_out, second_vectors)
    rates = (RATE_MATRIX, RATE_MATRIX, RATE_MATRIX, RATE_DENSE, RATE_MATRIX, RATE_MATRIX, RATE_VECTOR)
    decays = (WEIGHT_DECAY, WEIGHT_DECAY, WEIGHT_DECAY, WEIGHT_DECAY, WEIGHT_DECAY, WEIGHT_DECAY, 0.0)
    updated = [adam_update(parameter_set[slot], summed_total[slot], firsts[slot], seconds[slot], rates[slot], decays[slot]) for slot in range(7)]
    output = output_list.reshape(TOKENS, D)
    input_grad = incoming_gradient.reshape(TOKENS, D)
    return (output, input_grad, updated[0][0], updated[1][0], updated[2][0], updated[3][0], updated[4][0], updated[5][0], updated[6][0], updated[0][1], updated[1][1], updated[2][1], updated[3][1], updated[4][1], updated[5][1], updated[6][1], updated[0][2], updated[1][2], updated[2][2], updated[3][2], updated[4][2], updated[5][2], updated[6][2])
```

```python
import jax
import jax.numpy as jnp
from jax import lax
from jax.experimental import pallas as pl
from jax.experimental.pallas import tpu as pltpu
from jax.sharding import PartitionSpec as P

HEAD_DIM = 64
ROT = 16
STEP = 10


NORM_EPS = 1e-05
BETA_FIRST = 0.9
BETA_SECOND = 0.95
ADAM_EPS = 1e-08
WEIGHT_DECAY = 0.01
RATE_MATRIX = 0.04
RATE_DENSE = 0.2
RATE_VECTOR = 0.5
MASKED = -1000000000.0


def layout(lengths, offsets, total_rows):
    row_ids = jnp.arange(total_rows, dtype=jnp.int32)
    inside = (
        (row_ids[:, None] >= offsets[None, :])
        & (row_ids[:, None] < offsets[None, :] + lengths[None, :])
    ).astype(jnp.int32)
    slot_ids = jnp.arange(lengths.shape[0], dtype=jnp.int32)
    member = jnp.sum(inside, axis=1)
    segment = jnp.where(
        member > 0, jnp.sum(inside * slot_ids[None, :], axis=1), lengths.shape[0] + row_ids
    )
    position = jnp.where(member > 0, row_ids - jnp.sum(inside * offsets[None, :], axis=1), 0)
    return (segment, position)


LANES = 128
Q_BLOCK = 256
K_BLOCK = 512
INV_SQRT2 = 0.7071067811865476
INV_SQRT_2PI = 0.3989422804014327


def dot_nn(left, right):
    return lax.dot_general(
        left, right, (((1,), (0,)), ((), ())), preferred_element_type=jnp.float32
    )


def dot_nt(left, right):
    return lax.dot_general(
        left, right, (((1,), (1,)), ((), ())), preferred_element_type=jnp.float32
    )


def dot_tn(left, right):
    return lax.dot_general(
        left, right, (((0,), (0,)), ((), ())), preferred_element_type=jnp.float32
    )


def rotary_tables(position):
    half = ROT // 2
    lane = jnp.arange(LANES, dtype=jnp.int32) % HEAD_DIM
    freq = 10000.0 ** (-2.0 * (lane % half).astype(jnp.float32) / ROT)
    angle = position.astype(jnp.float32)[:, None] * freq[None, :]
    cosine, sine = jnp.cos(angle), jnp.sin(angle)
    return (
        jnp.where(lane < ROT, cosine, 1.0),
        jnp.where(lane < half, -sine, 0.0),
        jnp.where((lane >= half) & (lane < ROT), sine, 0.0),
    )


def turn(values, keep, ahead, behind):
    half = ROT // 2
    return (
        values * keep
        + pltpu.roll(values, LANES - half, 1) * ahead
        + pltpu.roll(values, half, 1) * behind
    )


def attention_kernel(
    first_ref, q_ref, k_ref, v_ref, do_ref, qkeep_ref, qahead_ref, qback_ref,
    keep_ref, ahead_ref, back_ref,
    out_ref, gq_ref, gk_ref, gv_ref,
    k_low, v_low, scores, pulls, gk_sum, gv_sum,
):
    block = pl.program_id(1)
    rows = k_ref.shape[0]
    q_rows = q_ref.shape[0]
    k_rows = min(K_BLOCK, rows)
    scale = HEAD_DIM ** (-0.5)

    @pl.when(block == 0)
    def _():
        k_low[...] = turn(
            k_ref[...], keep_ref[...], ahead_ref[...], back_ref[...]
        ).astype(jnp.bfloat16)
        v_low[...] = v_ref[...].astype(jnp.bfloat16)
        gk_sum[...] = jnp.zeros_like(gk_sum)
        gv_sum[...] = jnp.zeros_like(gv_sum)

    lane = lax.broadcasted_iota(jnp.int32, (q_rows, LANES), 1)
    q_low = turn(q_ref[...], qkeep_ref[...], qahead_ref[...], qback_ref[...])
    q_low = q_low.astype(jnp.bfloat16).astype(jnp.float32) * scale
    do_low = do_ref[...].astype(jnp.float32)
    mine = (lane < HEAD_DIM, lane >= HEAD_DIM)
    q_of = [jnp.where(m, q_low, 0.0).astype(jnp.bfloat16) for m in mine]
    do_of = [jnp.where(m, do_low, 0.0).astype(jnp.bfloat16) for m in mine]
    q_both = jnp.concatenate(q_of, axis=0)
    do_both = jnp.concatenate(do_of, axis=0)
    first = first_ref[...]
    row_id = block * q_rows + lax.broadcasted_iota(jnp.int32, (1, q_rows), 1)
    chunks = (block * q_rows + q_rows + k_rows - 1) // k_rows

    def at(chunk):
        return pl.ds(pl.multiple_of(chunk * k_rows, k_rows), k_rows)

    def score_step(chunk, tops):
        key_id = chunk * k_rows + lax.broadcasted_iota(jnp.int32, (k_rows, q_rows), 0)
        allowed = (key_id >= first) & (key_id <= row_id)
        new = []
        for h in range(2):
            block_scores = jnp.where(allowed, dot_nt(k_low[at(chunk), :], q_of[h]), MASKED)
            scores[h, at(chunk), :] = block_scores
            new.append(jnp.maximum(tops[h], jnp.max(block_scores, axis=0, keepdims=True)))
        return tuple(new)

    low_row = jnp.full((1, q_rows), MASKED, jnp.float32)
    tops = lax.fori_loop(0, chunks, score_step, (low_row, low_row))

    def weight_step(chunk, sums):
        new = []
        for h in range(2):
            exps = jnp.exp(scores[h, at(chunk), :] - tops[h])
            pull = dot_nt(v_low[at(chunk), :], do_of[h])
            scores[h, at(chunk), :] = exps
            pulls[h, at(chunk), :] = pull
            new.append(sums[2 * h] + jnp.sum(exps, axis=0, keepdims=True))
            new.append(sums[2 * h + 1] + jnp.sum(exps * pull, axis=0, keepdims=True))
        return tuple(new)

    zero_row = jnp.zeros((1, q_rows), jnp.float32)
    sums = lax.fori_loop(0, chunks, weight_step, (zero_row,) * 4)
    shares = [1.0 / sums[2 * h] for h in range(2)]
    centres = [sums[2 * h + 1] * shares[h] for h in range(2)]

    def gradient_step(chunk, carry):
        new = []
        lows, grads = [], []
        for h in range(2):
            probs = scores[h, at(chunk), :] * shares[h]
            lows.append(probs.astype(jnp.bfloat16))
            grads.append((probs * (pulls[h, at(chunk), :] - centres[h])).astype(jnp.bfloat16))
            new.append(carry[2 * h] + dot_tn(v_low[at(chunk), :], lows[h]))
            new.append(carry[2 * h + 1] + dot_tn(k_low[at(chunk), :], grads[h]))
        gv_sum[at(chunk), :] += dot_nn(jnp.concatenate(lows, axis=1), do_both)
        gk_sum[at(chunk), :] += dot_nn(jnp.concatenate(grads, axis=1), q_both)
        return tuple(new)

    zero_block = jnp.zeros((LANES, q_rows), jnp.float32)
    out_one, gq_one, out_two, gq_two = lax.fori_loop(
        0, chunks, gradient_step, (zero_block,) * 4
    )
    upper = lax.broadcasted_iota(jnp.int32, (LANES, q_rows), 0) < HEAD_DIM
    out_ref[...] = jnp.where(upper, out_one, out_two).T.astype(jnp.bfloat16)
    gq = jnp.where(upper, gq_one, gq_two).T * scale
    gq_ref[...] = turn(gq, qkeep_ref[...], -qahead_ref[...], -qback_ref[...]).astype(jnp.bfloat16)

    @pl.when(block == pl.num_programs(1) - 1)
    def _():
        gk_ref[...] = turn(
            gk_sum[...], keep_ref[...], -ahead_ref[...], -back_ref[...]
        ).astype(jnp.bfloat16)
        gv_ref[...] = gv_sum[...].astype(jnp.bfloat16)


def attention(first_row, lin, grad_attended, tables):
    rows, cols = grad_attended.shape
    pairs = cols // LANES
    q_rows = min(Q_BLOCK, rows)
    blocks = rows // q_rows
    tall = lambda shift: pl.BlockSpec((rows, LANES), lambda p, b: (0, p + shift))
    here = pl.BlockSpec((q_rows, LANES), lambda p, b: (b, p))
    table_here = pl.BlockSpec((q_rows, LANES), lambda p, b: (b, 0))
    table_tall = pl.BlockSpec((rows, LANES), lambda p, b: (0, 0))
    low = jax.ShapeDtypeStruct((rows, cols), jnp.bfloat16)
    return pl.pallas_call(
        attention_kernel,
        grid=(pairs, blocks),
        in_specs=[pl.BlockSpec((1, q_rows), lambda p, b: (0, b)), here, tall(pairs), tall(2 * pairs),
                  here] + [table_here] * 3 + [table_tall] * 3,
        out_specs=[here, here, tall(0), tall(0)],
        out_shape=[low] * 4,
        scratch_shapes=[
            pltpu.VMEM((rows, LANES), jnp.bfloat16),
            pltpu.VMEM((rows, LANES), jnp.bfloat16),
            pltpu.VMEM((2, rows, q_rows), jnp.float32),
            pltpu.VMEM((2, rows, q_rows), jnp.float32),
            pltpu.VMEM((rows, LANES), jnp.float32),
            pltpu.VMEM((rows, LANES), jnp.float32),
        ],
        compiler_params=pltpu.CompilerParams(vmem_limit_bytes=44 * 2**20),
        cost_estimate=pl.CostEstimate(
            flops=60 * 10**9, bytes_accessed=30 * 2**20, transcendentals=rows * rows * pairs
        ),
        name="attention",
    )(first_row[None, :], lin, lin, lin, grad_attended, *tables, *tables)


def hidden_kernel(normed_ref, dy_ref, in_ref, out_ref, bias_ref, act_ref, grad_ref):
    pre = dot_nn(normed_ref[...], in_ref[...]) + bias_ref[...]
    pull = dot_nn(dy_ref[...], out_ref[...])
    phi = 0.5 * (1.0 + lax.erf(pre * INV_SQRT2))
    act_ref[...] = (pre * phi).astype(jnp.bfloat16)
    slope = phi + pre * (INV_SQRT_2PI * jnp.exp(-0.5 * pre * pre))
    grad_ref[...] = (pull * slope).astype(jnp.bfloat16)


def hidden_units(normed, grad_rows, in_full, out_full, bias):
    rows, depth = normed.shape
    units = in_full.shape[1]
    tile_rows, tile_units = min(512, rows), min(512, units)
    row_spec = pl.BlockSpec((tile_rows, depth), lambda u, r: (r, 0))
    weight_spec = pl.BlockSpec((depth, tile_units), lambda u, r: (0, u))
    tile = pl.BlockSpec((tile_rows, tile_units), lambda u, r: (r, u))
    low = jax.ShapeDtypeStruct((rows, units), jnp.bfloat16)
    return pl.pallas_call(
        hidden_kernel,
        grid=(units // tile_units, rows // tile_rows),
        in_specs=[row_spec, row_spec, weight_spec, weight_spec,
                  pl.BlockSpec((1, tile_units), lambda u, r: (0, u))],
        out_specs=[tile, tile],
        out_shape=[low, low],
        compiler_params=pltpu.CompilerParams(vmem_limit_bytes=40 * 2**20),
        cost_estimate=pl.CostEstimate(
            flops=4 * rows * depth * units, bytes_accessed=40 * 2**20,
            transcendentals=2 * rows * units,
        ),
        name="hidden_units",
    )(normed, grad_rows, in_full, out_full, bias[None, :])


def adam_update(weight_matrix, grad, first, second, rate, decay):
    first = BETA_FIRST * first + (1.0 - BETA_FIRST) * grad
    second = BETA_SECOND * second + (1.0 - BETA_SECOND) * grad * grad
    fixed_first = first / (1.0 - BETA_FIRST**STEP)
    fixed_second = second / (1.0 - BETA_SECOND**STEP)
    weight_matrix = weight_matrix - rate * (
        fixed_first / (jnp.sqrt(fixed_second) + ADAM_EPS) + decay * weight_matrix
    )
    return (first, second, weight_matrix)


def shards(
    tokens,
    cotangent,
    sequence_lengths,
    sequence_starts,
    weight_query,
    weight_key,
    weight_value,
    weight_dense,
    weight_in,
    weight_out,
    vectors,
    first_query,
    first_key,
    first_value,
    first_dense,
    first_in,
    first_out,
    first_vectors,
    second_query,
    second_key,
    second_value,
    second_dense,
    second_in,
    second_out,
    second_vectors,
):
    tensor_size = lax.axis_size("tensor")
    tensor_rank = lax.axis_index("tensor")
    shard_rows, model_width = tokens.shape
    all_rows = shard_rows * tensor_size
    segment, position = layout(sequence_lengths[0], sequence_starts[0], all_rows)
    row_ids = jnp.arange(all_rows, dtype=jnp.int32)
    first_row = jnp.where(segment < sequence_lengths.shape[1], row_ids - position, row_ids)
    masters = (weight_query, weight_key, weight_value, weight_dense, weight_in, weight_out, vectors)
    low = jnp.bfloat16
    swap = [(0, 1), (1, 0)]

    def both_rows(mine):
        if tensor_size != 2:
            return lax.all_gather(mine, "tensor", axis=0, tiled=True)
        other = lax.ppermute(mine, "tensor", swap)
        rows = jnp.zeros((all_rows, model_width), mine.dtype)
        rows = lax.dynamic_update_slice(rows, mine, (tensor_rank * shard_rows, 0))
        return lax.dynamic_update_slice(rows, other, ((1 - tensor_rank) * shard_rows, 0))

    def summed_rows(part):
        if tensor_size != 2:
            return lax.psum_scatter(part, "tensor", scatter_dimension=0, tiled=True)
        mine = lax.dynamic_slice_in_dim(part, tensor_rank * shard_rows, shard_rows, 0)
        theirs = lax.dynamic_slice_in_dim(part, (1 - tensor_rank) * shard_rows, shard_rows, 0)
        return mine + lax.ppermute(theirs.astype(low), "tensor", swap).astype(jnp.float32)

    def gather(values):
        return lax.all_gather(values, "dp", axis=0, tiled=True)

    vector_copy = gather(vectors.astype(low)).astype(jnp.float32)
    in_full = gather(weight_in.astype(low))
    out_full = gather(weight_out.astype(low))
    attn_full = gather(
        jnp.concatenate([weight_query, weight_key, weight_value, weight_dense], axis=1).astype(low)
    )
    head_cols = weight_query.shape[1]
    hidden_cols = weight_in.shape[1]
    qkv_full = attn_full[:, : 3 * head_cols]
    dense_full = attn_full[:, 3 * head_cols :]
    gain_one, shift_one, gain_two, shift_two, bias_dense, bias_out = [
        vector_copy[:, column] for column in range(6)
    ]
    bias_qkv = lax.dynamic_slice_in_dim(
        vector_copy[:, 6:9].T, tensor_rank * head_cols, head_cols, axis=1
    ).reshape(-1)
    bias_in = lax.dynamic_slice_in_dim(
        vector_copy[:, 9:].T.reshape(-1), tensor_rank * hidden_cols, hidden_cols
    )
    whole_rows = both_rows(tokens).astype(jnp.float32)
    grad_rows = both_rows(cotangent)
    centred = whole_rows - jnp.mean(whole_rows, axis=-1, keepdims=True)
    rstd = lax.rsqrt(jnp.mean(centred * centred, axis=-1, keepdims=True) + NORM_EPS)
    unit = centred * rstd
    normed_one = (unit * gain_one + shift_one).astype(low)
    normed_two = (unit * gain_two + shift_two).astype(low)

    activated, grad_pre = hidden_units(normed_two, grad_rows, in_full, out_full, bias_in)
    grad_in = dot_tn(normed_two, grad_pre).astype(low)
    grad_out = dot_tn(grad_rows, activated).astype(low)

    def spread(values):
        return lax.psum_scatter(values, "dp", scatter_dimension=0, tiled=True)

    sum_in = spread(grad_in)
    sum_out = spread(grad_out)
    grad_two = dot_nt(grad_pre, in_full)

    lin = dot_nn(normed_one, qkv_full) + bias_qkv
    grad_attended = dot_nn(grad_rows, dense_full).astype(low)
    lin, grad_attended, grad_in, grad_out = lax.optimization_barrier(
        (lin, grad_attended, grad_in, grad_out)
    )
    attended, grad_query_lin, grad_key_lin, grad_value_lin = attention(
        first_row, lin, grad_attended, rotary_tables(position)
    )
    grad_qkv_lin = jnp.concatenate([grad_query_lin, grad_key_lin, grad_value_lin], axis=1)
    grad_qkv = dot_tn(normed_one, grad_qkv_lin).astype(low)
    sum_qkv = spread(grad_qkv)
    sum_dense = spread(dot_tn(grad_rows, attended).astype(low))
    mixed = dot_nt(attended, dense_full) + dot_nt(activated, out_full)
    output = (tokens.astype(jnp.float32) + summed_rows(mixed) + bias_dense + bias_out).astype(low)

    grad_one = dot_nt(grad_qkv_lin, qkv_full)
    pull = grad_one * gain_one + grad_two * gain_two
    grad_rows_part = rstd * (
        pull
        - jnp.mean(pull, axis=-1, keepdims=True)
        - unit * jnp.mean(pull * unit, axis=-1, keepdims=True)
    )
    input_grad = (cotangent.astype(jnp.float32) + summed_rows(grad_rows_part)).astype(low)

    def placed(values, total_len):
        return lax.dynamic_update_slice(
            jnp.zeros((total_len,), jnp.float32), values, (tensor_rank * values.shape[0],)
        )

    local_bias = jnp.sum(cotangent.astype(jnp.float32), axis=0)
    bias_grads = [
        placed(jnp.sum(part.astype(jnp.float32), axis=0), model_width)
        for part in (grad_query_lin, grad_key_lin, grad_value_lin)
    ]
    grad_bias_in = placed(jnp.sum(grad_pre.astype(jnp.float32), axis=0), hidden_cols * tensor_size)
    grad_vector = jnp.concatenate(
        [
            jnp.stack(
                [
                    jnp.sum(grad_one * unit, axis=0),
                    jnp.sum(grad_one, axis=0),
                    jnp.sum(grad_two * unit, axis=0),
                    jnp.sum(grad_two, axis=0),
                    local_bias,
                    local_bias,
                ]
                + bias_grads,
                axis=1,
            ),
            grad_bias_in.reshape(-1, model_width).T,
        ],
        axis=1,
    )
    vector_grad = lax.psum(spread(grad_vector), "tensor")
    sums = [sum_qkv[:, at * head_cols : (at + 1) * head_cols] for at in range(3)]
    grads = [part.astype(jnp.float32) for part in (*sums, sum_dense, sum_in, sum_out)]
    grads.append(vector_grad)
    firsts = (first_query, first_key, first_value, first_dense, first_in, first_out, first_vectors)
    seconds = (
        second_query,
        second_key,
        second_value,
        second_dense,
        second_in,
        second_out,
        second_vectors,
    )
    rates = (
        RATE_MATRIX,
        RATE_MATRIX,
        RATE_MATRIX,
        RATE_DENSE,
        RATE_MATRIX,
        RATE_MATRIX,
        RATE_VECTOR,
    )
    decays = (
        WEIGHT_DECAY,
        WEIGHT_DECAY,
        WEIGHT_DECAY,
        WEIGHT_DECAY,
        WEIGHT_DECAY,
        WEIGHT_DECAY,
        0.0,
    )
    updated = [
        adam_update(
            masters[slot], grads[slot], firsts[slot], seconds[slot], rates[slot], decays[slot]
        )
        for slot in range(7)
    ]
    return (
        output,
        input_grad,
        updated[0][0],
        updated[1][0],
        updated[2][0],
        updated[3][0],
        updated[4][0],
        updated[5][0],
        updated[6][0],
        updated[0][1],
        updated[1][1],
        updated[2][1],
        updated[3][1],
        updated[4][1],
        updated[5][1],
        updated[6][1],
        updated[0][2],
        updated[1][2],
        updated[2][2],
        updated[3][2],
        updated[4][2],
        updated[5][2],
        updated[6][2],
    )


def solution(mesh):
    in_specs = (
        P(("dp", "tensor"), None),
        P(("dp", "tensor"), None),
        P("dp", None),
        P("dp", None),
        P("dp", "tensor"),
        P("dp", "tensor"),
        P("dp", "tensor"),
        P("dp", "tensor"),
        P("dp", "tensor"),
        P("dp", "tensor"),
        P("dp", None),
        P("dp", "tensor"),
        P("dp", "tensor"),
        P("dp", "tensor"),
        P("dp", "tensor"),
        P("dp", "tensor"),
        P("dp", "tensor"),
        P("dp", None),
        P("dp", "tensor"),
        P("dp", "tensor"),
        P("dp", "tensor"),
        P("dp", "tensor"),
        P("dp", "tensor"),
        P("dp", "tensor"),
        P("dp", None),
    )
    out_specs = (
        P(("dp", "tensor"), None),
        P(("dp", "tensor"), None),
        P("dp", "tensor"),
        P("dp", "tensor"),
        P("dp", "tensor"),
        P("dp", "tensor"),
        P("dp", "tensor"),
        P("dp", "tensor"),
        P("dp", None),
        P("dp", "tensor"),
        P("dp", "tensor"),
        P("dp", "tensor"),
        P("dp", "tensor"),
        P("dp", "tensor"),
        P("dp", "tensor"),
        P("dp", None),
        P("dp", "tensor"),
        P("dp", "tensor"),
        P("dp", "tensor"),
        P("dp", "tensor"),
        P("dp", "tensor"),
        P("dp", "tensor"),
        P("dp", None),
    )
    return jax.shard_map(shards, mesh=mesh, in_specs=in_specs, out_specs=out_specs, check_vma=False)
```

```python
import jax
import jax.numpy as jnp
from jax import lax
from jax.experimental import pallas as pl
from jax.experimental.pallas import tpu as pltpu
from jax.sharding import PartitionSpec as P

HEAD_DIM = 64
ROT = 16
STEP = 10


NORM_EPS = 1e-05
BETA_FIRST = 0.9
BETA_SECOND = 0.95
ADAM_EPS = 1e-08
WEIGHT_DECAY = 0.01
RATE_MATRIX = 0.04
RATE_DENSE = 0.2
RATE_VECTOR = 0.5
MASKED = -1000000000.0


def layout(lengths, offsets, total_rows):
    row_ids = jnp.arange(total_rows, dtype=jnp.int32)
    inside = (
        (row_ids[:, None] >= offsets[None, :])
        & (row_ids[:, None] < offsets[None, :] + lengths[None, :])
    ).astype(jnp.int32)
    slot_ids = jnp.arange(lengths.shape[0], dtype=jnp.int32)
    member = jnp.sum(inside, axis=1)
    segment = jnp.where(
        member > 0, jnp.sum(inside * slot_ids[None, :], axis=1), lengths.shape[0] + row_ids
    )
    position = jnp.where(member > 0, row_ids - jnp.sum(inside * offsets[None, :], axis=1), 0)
    return (segment, position)


LANES = 128
Q_BLOCK = 256
K_BLOCK = 512
INV_SQRT2 = 0.7071067811865476
INV_SQRT_2PI = 0.3989422804014327


def dot_nn(left, right):
    return lax.dot_general(
        left, right, (((1,), (0,)), ((), ())), preferred_element_type=jnp.float32
    )


def dot_nt(left, right):
    return lax.dot_general(
        left, right, (((1,), (1,)), ((), ())), preferred_element_type=jnp.float32
    )


def dot_tn(left, right):
    return lax.dot_general(
        left, right, (((0,), (0,)), ((), ())), preferred_element_type=jnp.float32
    )


def rotary_tables(position):
    half = ROT // 2
    lane = jnp.arange(LANES, dtype=jnp.int32) % HEAD_DIM
    freq = 10000.0 ** (-2.0 * (lane % half).astype(jnp.float32) / ROT)
    angle = position.astype(jnp.float32)[:, None] * freq[None, :]
    cosine, sine = jnp.cos(angle), jnp.sin(angle)
    return (
        jnp.where(lane < ROT, cosine, 1.0),
        jnp.where(lane < half, -sine, 0.0),
        jnp.where((lane >= half) & (lane < ROT), sine, 0.0),
    )


def turn(values, keep, ahead, behind):
    half = ROT // 2
    return (
        values * keep
        + pltpu.roll(values, LANES - half, 1) * ahead
        + pltpu.roll(values, half, 1) * behind
    )


def attention_kernel(
    first_ref, q_ref, k_ref, v_ref, do_ref, qkeep_ref, qahead_ref, qback_ref,
    keep_ref, ahead_ref, back_ref,
    out_ref, gq_ref, gk_ref, gv_ref,
    k_low, v_low, scores, pulls, gk_sum, gv_sum,
):
    block = pl.program_id(1)
    rows = k_ref.shape[0]
    q_rows = q_ref.shape[0]
    k_rows = min(K_BLOCK, rows)
    scale = HEAD_DIM ** (-0.5)

    @pl.when(block == 0)
    def _():
        k_low[...] = turn(
            k_ref[...], keep_ref[...], ahead_ref[...], back_ref[...]
        ).astype(jnp.bfloat16)
        v_low[...] = v_ref[...].astype(jnp.bfloat16)
        gk_sum[...] = jnp.zeros_like(gk_sum)
        gv_sum[...] = jnp.zeros_like(gv_sum)

    lane = lax.broadcasted_iota(jnp.int32, (q_rows, LANES), 1)
    q_low = turn(q_ref[...], qkeep_ref[...], qahead_ref[...], qback_ref[...])
    q_low = q_low.astype(jnp.bfloat16).astype(jnp.float32) * scale
    do_low = do_ref[...].astype(jnp.float32)
    mine = (lane < HEAD_DIM, lane >= HEAD_DIM)
    q_of = [jnp.where(m, q_low, 0.0).astype(jnp.bfloat16) for m in mine]
    do_of = [jnp.where(m, do_low, 0.0).astype(jnp.bfloat16) for m in mine]
    q_both = jnp.concatenate(q_of, axis=0)
    do_both = jnp.concatenate(do_of, axis=0)
    first = first_ref[...]
    row_id = block * q_rows + lax.broadcasted_iota(jnp.int32, (1, q_rows), 1)
    chunks = (block * q_rows + q_rows + k_rows - 1) // k_rows

    def at(chunk):
        return pl.ds(pl.multiple_of(chunk * k_rows, k_rows), k_rows)

    def score_step(chunk, tops):
        key_id = chunk * k_rows + lax.broadcasted_iota(jnp.int32, (k_rows, q_rows), 0)
        allowed = (key_id >= first) & (key_id <= row_id)
        new = []
        for h in range(2):
            block_scores = jnp.where(allowed, dot_nt(k_low[at(chunk), :], q_of[h]), MASKED)
            scores[h, at(chunk), :] = block_scores
            new.append(jnp.maximum(tops[h], jnp.max(block_scores, axis=0, keepdims=True)))
        return tuple(new)

    low_row = jnp.full((1, q_rows), MASKED, jnp.float32)
    tops = lax.fori_loop(0, chunks, score_step, (low_row, low_row))

    def weight_step(chunk, sums):
        new = []
        for h in range(2):
            exps = jnp.exp(scores[h, at(chunk), :] - tops[h])
            pull = dot_nt(v_low[at(chunk), :], do_of[h])
            scores[h, at(chunk), :] = exps
            pulls[h, at(chunk), :] = pull
            new.append(sums[2 * h] + jnp.sum(exps, axis=0, keepdims=True))
            new.append(sums[2 * h + 1] + jnp.sum(exps * pull, axis=0, keepdims=True))
        return tuple(new)

    zero_row = jnp.zeros((1, q_rows), jnp.float32)
    sums = lax.fori_loop(0, chunks, weight_step, (zero_row,) * 4)
    shares = [1.0 / sums[2 * h] for h in range(2)]
    centres = [sums[2 * h + 1] * shares[h] for h in range(2)]

    def gradient_step(chunk, carry):
        new = []
        lows, grads = [], []
        for h in range(2):
            probs = scores[h, at(chunk), :] * shares[h]
            lows.append(probs.astype(jnp.bfloat16))
            grads.append((probs * (pulls[h, at(chunk), :] - centres[h])).astype(jnp.bfloat16))
            new.append(carry[2 * h] + dot_tn(v_low[at(chunk), :], lows[h]))
            new.append(carry[2 * h + 1] + dot_tn(k_low[at(chunk), :], grads[h]))
        gv_sum[at(chunk), :] += dot_nn(jnp.concatenate(lows, axis=1), do_both)
        gk_sum[at(chunk), :] += dot_nn(jnp.concatenate(grads, axis=1), q_both)
        return tuple(new)

    zero_block = jnp.zeros((LANES, q_rows), jnp.float32)
    out_one, gq_one, out_two, gq_two = lax.fori_loop(
        0, chunks, gradient_step, (zero_block,) * 4
    )
    upper = lax.broadcasted_iota(jnp.int32, (LANES, q_rows), 0) < HEAD_DIM
    out_ref[...] = jnp.where(upper, out_one, out_two).T.astype(jnp.bfloat16)
    gq = jnp.where(upper, gq_one, gq_two).T * scale
    gq_ref[...] = turn(gq, qkeep_ref[...], -qahead_ref[...], -qback_ref[...]).astype(jnp.bfloat16)

    @pl.when(block == pl.num_programs(1) - 1)
    def _():
        gk_ref[...] = turn(
            gk_sum[...], keep_ref[...], -ahead_ref[...], -back_ref[...]
        ).astype(jnp.bfloat16)
        gv_ref[...] = gv_sum[...].astype(jnp.bfloat16)


def attention(first_row, lin, grad_attended, tables):
    rows, cols = grad_attended.shape
    pairs = cols // LANES
    q_rows = min(Q_BLOCK, rows)
    blocks = rows // q_rows
    tall = lambda shift: pl.BlockSpec((rows, LANES), lambda p, b: (0, p + shift))
    here = pl.BlockSpec((q_rows, LANES), lambda p, b: (b, p))
    table_here = pl.BlockSpec((q_rows, LANES), lambda p, b: (b, 0))
    table_tall = pl.BlockSpec((rows, LANES), lambda p, b: (0, 0))
    low = jax.ShapeDtypeStruct((rows, cols), jnp.bfloat16)
    return pl.pallas_call(
        attention_kernel,
        grid=(pairs, blocks),
        in_specs=[pl.BlockSpec((1, q_rows), lambda p, b: (0, b)), here, tall(pairs), tall(2 * pairs),
                  here] + [table_here] * 3 + [table_tall] * 3,
        out_specs=[here, here, tall(0), tall(0)],
        out_shape=[low] * 4,
        scratch_shapes=[
            pltpu.VMEM((rows, LANES), jnp.bfloat16),
            pltpu.VMEM((rows, LANES), jnp.bfloat16),
            pltpu.VMEM((2, rows, q_rows), jnp.float32),
            pltpu.VMEM((2, rows, q_rows), jnp.float32),
            pltpu.VMEM((rows, LANES), jnp.float32),
            pltpu.VMEM((rows, LANES), jnp.float32),
        ],
        compiler_params=pltpu.CompilerParams(vmem_limit_bytes=44 * 2**20),
        cost_estimate=pl.CostEstimate(
            flops=60 * 10**9, bytes_accessed=30 * 2**20, transcendentals=rows * rows * pairs
        ),
        name="attention",
    )(first_row[None, :], lin, lin, lin, grad_attended, *tables, *tables)


def hidden_kernel(normed_ref, dy_ref, in_ref, out_ref, bias_ref, act_ref, grad_ref):
    pre = dot_nn(normed_ref[...], in_ref[...]) + bias_ref[...]
    pull = dot_nn(dy_ref[...], out_ref[...])
    phi = 0.5 * (1.0 + lax.erf(pre * INV_SQRT2))
    act_ref[...] = (pre * phi).astype(jnp.bfloat16)
    slope = phi + pre * (INV_SQRT_2PI * jnp.exp(-0.5 * pre * pre))
    grad_ref[...] = (pull * slope).astype(jnp.bfloat16)


def hidden_units(normed, grad_rows, in_full, out_full, bias):
    rows, depth = normed.shape
    units = in_full.shape[1]
    tile_rows, tile_units = min(512, rows), min(512, units)
    row_spec = pl.BlockSpec((tile_rows, depth), lambda u, r: (r, 0))
    weight_spec = pl.BlockSpec((depth, tile_units), lambda u, r: (0, u))
    tile = pl.BlockSpec((tile_rows, tile_units), lambda u, r: (r, u))
    low = jax.ShapeDtypeStruct((rows, units), jnp.bfloat16)
    return pl.pallas_call(
        hidden_kernel,
        grid=(units // tile_units, rows // tile_rows),
        in_specs=[row_spec, row_spec, weight_spec, weight_spec,
                  pl.BlockSpec((1, tile_units), lambda u, r: (0, u))],
        out_specs=[tile, tile],
        out_shape=[low, low],
        compiler_params=pltpu.CompilerParams(vmem_limit_bytes=40 * 2**20),
        cost_estimate=pl.CostEstimate(
            flops=4 * rows * depth * units, bytes_accessed=40 * 2**20,
            transcendentals=2 * rows * units,
        ),
        name="hidden_units",
    )(normed, grad_rows, in_full, out_full, bias[None, :])


def adam_update(weight_matrix, grad, first, second, rate, decay):
    first = BETA_FIRST * first + (1.0 - BETA_FIRST) * grad
    second = BETA_SECOND * second + (1.0 - BETA_SECOND) * grad * grad
    fixed_first = first / (1.0 - BETA_FIRST**STEP)
    fixed_second = second / (1.0 - BETA_SECOND**STEP)
    weight_matrix = weight_matrix - rate * (
        fixed_first / (jnp.sqrt(fixed_second) + ADAM_EPS) + decay * weight_matrix
    )
    return (first, second, weight_matrix)


def shards(
    tokens,
    cotangent,
    sequence_lengths,
    sequence_starts,
    weight_query,
    weight_key,
    weight_value,
    weight_dense,
    weight_in,
    weight_out,
    vectors,
    first_query,
    first_key,
    first_value,
    first_dense,
    first_in,
    first_out,
    first_vectors,
    second_query,
    second_key,
    second_value,
    second_dense,
    second_in,
    second_out,
    second_vectors,
):
    tensor_size = lax.axis_size("tensor")
    tensor_rank = lax.axis_index("tensor")
    shard_rows, model_width = tokens.shape
    all_rows = shard_rows * tensor_size
    segment, position = layout(sequence_lengths[0], sequence_starts[0], all_rows)
    row_ids = jnp.arange(all_rows, dtype=jnp.int32)
    first_row = jnp.where(segment < sequence_lengths.shape[1], row_ids - position, row_ids)
    masters = (weight_query, weight_key, weight_value, weight_dense, weight_in, weight_out, vectors)
    low = jnp.bfloat16
    swap = [(0, 1), (1, 0)]

    def both_rows(mine):
        if tensor_size != 2:
            return lax.all_gather(mine, "tensor", axis=0, tiled=True)
        other = lax.ppermute(mine, "tensor", swap)
        rows = jnp.zeros((all_rows, model_width), mine.dtype)
        rows = lax.dynamic_update_slice(rows, mine, (tensor_rank * shard_rows, 0))
        return lax.dynamic_update_slice(rows, other, ((1 - tensor_rank) * shard_rows, 0))

    def summed_rows(part):
        if tensor_size != 2:
            return lax.psum_scatter(part, "tensor", scatter_dimension=0, tiled=True)
        mine = lax.dynamic_slice_in_dim(part, tensor_rank * shard_rows, shard_rows, 0)
        theirs = lax.dynamic_slice_in_dim(part, (1 - tensor_rank) * shard_rows, shard_rows, 0)
        return mine + lax.ppermute(theirs.astype(low), "tensor", swap).astype(jnp.float32)

    def gather(values):
        return lax.all_gather(values, "dp", axis=0, tiled=True)

    vector_copy = gather(vectors.astype(low)).astype(jnp.float32)
    in_full = gather(weight_in.astype(low))
    out_full = gather(weight_out.astype(low))
    attn_full = gather(
        jnp.concatenate([weight_query, weight_key, weight_value, weight_dense], axis=1).astype(low)
    )
    head_cols = weight_query.shape[1]
    hidden_cols = weight_in.shape[1]
    qkv_full = attn_full[:, : 3 * head_cols]
    dense_full = attn_full[:, 3 * head_cols :]
    gain_one, shift_one, gain_two, shift_two, bias_dense, bias_out = [
        vector_copy[:, column] for column in range(6)
    ]
    bias_qkv = lax.dynamic_slice_in_dim(
        vector_copy[:, 6:9].T, tensor_rank * head_cols, head_cols, axis=1
    ).reshape(-1)
    bias_in = lax.dynamic_slice_in_dim(
        vector_copy[:, 9:].T.reshape(-1), tensor_rank * hidden_cols, hidden_cols
    )
    whole_rows = both_rows(tokens).astype(jnp.float32)
    grad_rows = both_rows(cotangent)
    centred = whole_rows - jnp.mean(whole_rows, axis=-1, keepdims=True)
    rstd = lax.rsqrt(jnp.mean(centred * centred, axis=-1, keepdims=True) + NORM_EPS)
    unit = centred * rstd
    normed_one = (unit * gain_one + shift_one).astype(low)
    normed_two = (unit * gain_two + shift_two).astype(low)

    activated, grad_pre = hidden_units(normed_two, grad_rows, in_full, out_full, bias_in)
    grad_in = dot_tn(normed_two, grad_pre).astype(low)
    grad_out = dot_tn(grad_rows, activated).astype(low)

    def spread(values):
        return lax.psum_scatter(values, "dp", scatter_dimension=0, tiled=True)

    sum_in = spread(grad_in)
    sum_out = spread(grad_out)
    grad_two = dot_nt(grad_pre, in_full)

    lin = dot_nn(normed_one, qkv_full) + bias_qkv
    grad_attended = dot_nn(grad_rows, dense_full).astype(low)
    lin, grad_attended, grad_in, grad_out = lax.optimization_barrier(
        (lin, grad_attended, grad_in, grad_out)
    )
    attended, grad_query_lin, grad_key_lin, grad_value_lin = attention(
        first_row, lin, grad_attended, rotary_tables(position)
    )
    attended, grad_query_lin, grad_key_lin, grad_value_lin, sum_in, sum_out = (
        lax.optimization_barrier(
            (attended, grad_query_lin, grad_key_lin, grad_value_lin, sum_in, sum_out)
        )
    )
    grad_qkv_lin = jnp.concatenate([grad_query_lin, grad_key_lin, grad_value_lin], axis=1)
    grad_qkv = dot_tn(normed_one, grad_qkv_lin).astype(low)
    sum_qkv = spread(grad_qkv)
    sum_dense = spread(dot_tn(grad_rows, attended).astype(low))
    mixed = dot_nt(attended, dense_full) + dot_nt(activated, out_full)
    output = (tokens.astype(jnp.float32) + summed_rows(mixed) + bias_dense + bias_out).astype(low)

    grad_one = dot_nt(grad_qkv_lin, qkv_full)
    pull = grad_one * gain_one + grad_two * gain_two
    grad_rows_part = rstd * (
        pull
        - jnp.mean(pull, axis=-1, keepdims=True)
        - unit * jnp.mean(pull * unit, axis=-1, keepdims=True)
    )
    input_grad = (cotangent.astype(jnp.float32) + summed_rows(grad_rows_part)).astype(low)

    def placed(values, total_len):
        return lax.dynamic_update_slice(
            jnp.zeros((total_len,), jnp.float32), values, (tensor_rank * values.shape[0],)
        )

    local_bias = jnp.sum(cotangent.astype(jnp.float32), axis=0)
    bias_grads = [
        placed(jnp.sum(part.astype(jnp.float32), axis=0), model_width)
        for part in (grad_query_lin, grad_key_lin, grad_value_lin)
    ]
    grad_bias_in = placed(jnp.sum(grad_pre.astype(jnp.float32), axis=0), hidden_cols * tensor_size)
    grad_vector = jnp.concatenate(
        [
            jnp.stack(
                [
                    jnp.sum(grad_one * unit, axis=0),
                    jnp.sum(grad_one, axis=0),
                    jnp.sum(grad_two * unit, axis=0),
                    jnp.sum(grad_two, axis=0),
                    local_bias,
                    local_bias,
                ]
                + bias_grads,
                axis=1,
            ),
            grad_bias_in.reshape(-1, model_width).T,
        ],
        axis=1,
    )
    vector_grad = lax.psum(spread(grad_vector), "tensor")
    sums = [sum_qkv[:, at * head_cols : (at + 1) * head_cols] for at in range(3)]
    grads = [part.astype(jnp.float32) for part in (*sums, sum_dense, sum_in, sum_out)]
    grads.append(vector_grad)
    firsts = (first_query, first_key, first_value, first_dense, first_in, first_out, first_vectors)
    seconds = (
        second_query,
        second_key,
        second_value,
        second_dense,
        second_in,
        second_out,
        second_vectors,
    )
    rates = (
        RATE_MATRIX,
        RATE_MATRIX,
        RATE_MATRIX,
        RATE_DENSE,
        RATE_MATRIX,
        RATE_MATRIX,
        RATE_VECTOR,
    )
    decays = (
        WEIGHT_DECAY,
        WEIGHT_DECAY,
        WEIGHT_DECAY,
        WEIGHT_DECAY,
        WEIGHT_DECAY,
        WEIGHT_DECAY,
        0.0,
    )
    updated = [
        adam_update(
            masters[slot], grads[slot], firsts[slot], seconds[slot], rates[slot], decays[slot]
        )
        for slot in range(7)
    ]
    return (
        output,
        input_grad,
        updated[0][0],
        updated[1][0],
        updated[2][0],
        updated[3][0],
        updated[4][0],
        updated[5][0],
        updated[6][0],
        updated[0][1],
        updated[1][1],
        updated[2][1],
        updated[3][1],
        updated[4][1],
        updated[5][1],
        updated[6][1],
        updated[0][2],
        updated[1][2],
        updated[2][2],
        updated[3][2],
        updated[4][2],
        updated[5][2],
        updated[6][2],
    )


def solution(mesh):
    in_specs = (
        P(("dp", "tensor"), None),
        P(("dp", "tensor"), None),
        P("dp", None),
        P("dp", None),
        P("dp", "tensor"),
        P("dp", "tensor"),
        P("dp", "tensor"),
        P("dp", "tensor"),
        P("dp", "tensor"),
        P("dp", "tensor"),
        P("dp", None),
        P("dp", "tensor"),
        P("dp", "tensor"),
        P("dp", "tensor"),
        P("dp", "tensor"),
        P("dp", "tensor"),
        P("dp", "tensor"),
        P("dp", None),
        P("dp", "tensor"),
        P("dp", "tensor"),
        P("dp", "tensor"),
        P("dp", "tensor"),
        P("dp", "tensor"),
        P("dp", "tensor"),
        P("dp", None),
    )
    out_specs = (
        P(("dp", "tensor"), None),
        P(("dp", "tensor"), None),
        P("dp", "tensor"),
        P("dp", "tensor"),
        P("dp", "tensor"),
        P("dp", "tensor"),
        P("dp", "tensor"),
        P("dp", "tensor"),
        P("dp", None),
        P("dp", "tensor"),
        P("dp", "tensor"),
        P("dp", "tensor"),
        P("dp", "tensor"),
        P("dp", "tensor"),
        P("dp", "tensor"),
        P("dp", None),
        P("dp", "tensor"),
        P("dp", "tensor"),
        P("dp", "tensor"),
        P("dp", "tensor"),
        P("dp", "tensor"),
        P("dp", "tensor"),
        P("dp", None),
    )
    return jax.shard_map(shards, mesh=mesh, in_specs=in_specs, out_specs=out_specs, check_vma=False)
```
